32 devices in a mesh: seq: 16 (over z, y, x), head: 2 (over core).
Axes of the slice: x: 2, y: 2, z: 4, core: 2. Of those that a mesh axis runs over, the one named last changes fastest.
Arguments:
- query_rows: bfloat16 [8192, 8, 128], P('seq', 'head'), may hold values from -8 to 8
- key_rows: bfloat16 [8192, 8, 128], P('seq', 'head'), may hold values from -8 to 8
- value_rows: bfloat16 [8192, 8, 128], P('seq', 'head'), may hold values from -8 to 8
- out_weight: bfloat16 [8, 128, 2048], P('head'), may hold values from -0.1875 to 0.1875
Outputs:
- layer_out: bfloat16 [8192, 2048], P('seq', 'head')
The draws below stay inside these ranges and needn't reach their ends.
All inputs are finite; a program needn't handle non-finite values.
Results may differ from the reference program's by a relative error of at most 0.015.
Values may be sent and summed in bfloat16 or wider, within the bound.
A program may use at most 64 MiB of HBM per device.

```python
import jax
import jax.numpy as jnp
from jax import lax

D = 2048
HEADS = 8
DH = 128
BLOCK = 128
TOK_DEV = 512
TOKENS = 8192
LEVELS = 4
N_SEQ = 16
N_HEAD = 2


def layered_rows(key, salt):
    streams = jax.random.split(jax.random.fold_in(key, salt), 7)
    values = 1.1 * jax.random.normal(streams[0], (TOKENS, HEADS, DH), jnp.float32)
    positions = jnp.arange(TOKENS, dtype=jnp.int32)
    for order, span_bits in enumerate((3, 4, 5, 6, 7, 8)):
        broad = jax.random.normal(streams[order + 1], ((TOKENS >> span_bits) + 1, HEADS, DH), jnp.float32)
        values = values + 0.775 * broad[positions >> span_bits]
    return jnp.clip(values, -8.0, 8.0)


def draw_query_rows(key, part):
    values = layered_rows(key, 11)
    return values.astype(jnp.bfloat16)


def draw_key_rows(key, part):
    values = layered_rows(key, 13)
    return values.astype(jnp.bfloat16)


def draw_value_rows(key, part):
    streams = jax.random.split(jax.random.fold_in(key, 17), 7)
    values = jax.random.normal(streams[0], (TOKENS, HEADS, DH), jnp.float32)
    positions = jnp.arange(TOKENS, dtype=jnp.int32)
    for order, span_bits in enumerate((4, 6, 8, 10, 12, 14)):
        broad = jax.random.normal(streams[order + 1], ((TOKENS >> span_bits) + 1, HEADS, DH), jnp.float32)
        values = values + 0.6 * broad[positions >> span_bits]
    return jnp.clip(values, -8.0, 8.0).astype(jnp.bfloat16)


def levels(stream_key, shape, shards, low, top_value):
    loudness = 1.0
    for dim, parts in shards:
        heights = jax.random.uniform(jax.random.fold_in(jax.random.fold_in(stream_key, 6), dim), (parts,), jnp.float32, low / len(shards), top_value / len(shards))
        loudness = loudness * jnp.repeat(jnp.exp(heights), shape[dim] // parts).reshape((-1,) + (1,) * (len(shape) - 1 - dim))
    return loudness


def gaussian(rng, extent, scale, most, pieces=(), kind=jnp.bfloat16):
    loudness = levels(rng, extent, pieces, -0.22, 0.18) if pieces else 1.0
    entries = jax.random.normal(rng, extent, jnp.float32) * scale * loudness
    return jnp.minimum(jnp.maximum(entries, -most), most).astype(kind)


def setup_inputs(seed: int = 0) -> dict:
    key_list = jax.random.split(jax.random.key(seed), 5)
    query_rows = draw_query_rows(jax.random.fold_in(key_list[4], 71), 0)
    key_rows = draw_key_rows(jax.random.fold_in(key_list[4], 71), 0)
    value_rows = draw_value_rows(jax.random.fold_in(key_list[4], 71), 0)
    out_weight = gaussian(key_list[3], (HEADS, DH, D), (HEADS * DH) ** -0.5, 0.1875, ((0, 2),))
    return {"query_rows": query_rows, "key_rows": key_rows, "value_rows": value_rows, "out_weight": out_weight}


def coarsen(source, level_index, average):
    if level_index == 0:
        return source
    count = source.shape[0] >> level_index
    grouped = source.astype(jnp.float32).reshape((count, 1 << level_index) + source.shape[1:])
    summed = jnp.sum(grouped, axis=1)
    if average:
        summed = summed / float(1 << level_index)
    return summed.astype(jnp.bfloat16)


def slot_targets(block_index, level_index):
    if level_index == 0:
        return [block_index - 1, block_index, block_index + 1]
    return [block_index - 2, block_index + 2, jnp.where(block_index % 2 == 0, block_index + 3, block_index - 3)]


def level_terms(query_head, key_head, value_head, level_index, scale):
    coarse_query = coarsen(query_head, level_index, True)
    coarse_key = coarsen(key_head, level_index, True)
    coarse_value = coarsen(value_head, level_index, False)
    total_blocks = coarse_query.shape[0] // BLOCK
    query_blocks = coarse_query.reshape(total_blocks, BLOCK, -1)
    key_blocks = coarse_key.reshape(total_blocks, BLOCK, -1)
    value_blocks = coarse_value.reshape(total_blocks, BLOCK, -1)
    block_index = jnp.arange(total_blocks, dtype=jnp.int32)
    targets = slot_targets(block_index, level_index)
    picked_keys = jnp.concatenate([key_blocks[jnp.clip(target, 0, total_blocks - 1)] for target in targets], axis=1)
    picked_values = jnp.concatenate([value_blocks[jnp.clip(target, 0, total_blocks - 1)] for target in targets], axis=1)
    valid = jnp.concatenate([jnp.repeat(((target >= 0) & (target < total_blocks))[:, None], BLOCK, axis=1) for target in targets], axis=1)
    scores = jnp.einsum("nqd,nkd->nqk", query_blocks.astype(jnp.float32), picked_keys.astype(jnp.float32)) * scale
    scores = jnp.where(valid[:, None, :], scores, -jnp.inf)
    row_peak = jnp.max(scores, axis=2, keepdims=True)
    weights = jnp.exp(scores - row_peak)
    denominator = float(1 << level_index) * jnp.sum(weights, axis=2)
    rounded = lax.optimization_barrier(weights.astype(jnp.bfloat16))
    numerator = jnp.einsum("nqk,nkd->nqd", rounded.astype(jnp.float32), picked_values.astype(jnp.float32))
    count = total_blocks * BLOCK
    return row_peak.reshape(count), numerator.reshape(count, -1), denominator.reshape(count)


def reference(query_rows, key_rows, value_rows, out_weight):
    scale = float(DH) ** -0.5

    def one_head(operands):
        query_head, key_head, value_head = operands
        expanded = []
        for level_index in range(LEVELS + 1):
            row_peak, numerator, denominator = level_terms(query_head, key_head, value_head, level_index, scale)
            factor = 1 << level_index
            expanded.append((jnp.repeat(row_peak, factor, axis=0), jnp.repeat(numerator, factor, axis=0), jnp.repeat(denominator, factor, axis=0)))
        overall = expanded[0][0]
        for entry in expanded[1:]:
            overall = jnp.maximum(overall, entry[0])
        weighted = jnp.zeros((TOKENS, DH), jnp.float32)
        total_weight = jnp.zeros((TOKENS,), jnp.float32)
        for part_peak, numerator, denominator in expanded:
            level_factor = jnp.exp(part_peak - overall)
            weighted = weighted + level_factor[:, None] * numerator
            total_weight = total_weight + level_factor * denominator
        return (weighted / total_weight[:, None]).astype(jnp.bfloat16)

    stacked = (jnp.transpose(query_rows, (1, 0, 2)), jnp.transpose(key_rows, (1, 0, 2)), jnp.transpose(value_rows, (1, 0, 2)))
    per_head = lax.map(one_head, stacked)
    attended = jnp.transpose(per_head, (1, 0, 2)).reshape(N_SEQ, TOK_DEV, N_HEAD, (HEADS // N_HEAD) * DH)
    grouped_weight = out_weight.reshape(N_HEAD, (HEADS // N_HEAD) * DH, D)

    def project(row_block):
        total = jnp.zeros((TOK_DEV, D), jnp.float32)
        for group in range(N_HEAD):
            partial_value = jnp.dot(row_block[:, group], grouped_weight[group], preferred_element_type=jnp.float32).astype(jnp.bfloat16)
            partial_value = lax.optimization_barrier(partial_value)
            total = total + partial_value.astype(jnp.float32)
        return total.astype(jnp.bfloat16)

    return lax.map(project, attended).reshape(TOKENS, D)
```

```python
import functools

import jax
import jax.numpy as jnp
from jax import lax
from jax.experimental import pallas as pl
from jax.experimental.pallas import tpu as pltpu
from jax.sharding import PartitionSpec as P

BLOCK = 128


def partner_2(value, axis, distance):
    mask = 2**distance
    pairs = [(source, source ^ mask) for source in range(lax.axis_size(axis))]
    return lax.ppermute(value, axis, pairs)


def shifted(value, axis, steps):
    count = lax.axis_size(axis)
    initial, last = (max(0, -steps), min(count, count - steps))
    return lax.ppermute(value, axis, [(source, source + steps) for source in range(initial, last)])


def coarsen(source, level_index, average):
    count = source.shape[0] >> level_index
    grouped = source.astype(jnp.float32).reshape((count, 1 << level_index) + source.shape[1:])
    summed = jnp.sum(grouped, axis=1)
    if average:
        summed = summed / float(1 << level_index)
    return summed.astype(jnp.bfloat16)


def slot_targets(block_index, level_index):
    if level_index == 0:
        return [block_index - 1, block_index, block_index + 1]
    return [
        block_index - 2,
        block_index + 2,
        jnp.where(block_index % 2 == 0, block_index + 3, block_index - 3),
    ]


def slot_masks(block_index, block_total, level_index, width):
    targets = slot_targets(block_index, level_index)
    return jnp.concatenate(
        [
            jnp.repeat(((target >= 0) & (target < block_total))[:, None], width, axis=1)
            for target in targets
        ],
        axis=1,
    )


def level_attend(query_blocks, key_blocks, value_blocks, valid, level_index, scale):
    scores = (
        jnp.einsum("nqhd,nkhd->nhqk", query_blocks, key_blocks, preferred_element_type=jnp.float32)
        * scale
    )
    scores = jnp.where(valid[:, None, None, :], scores, -jnp.inf)
    row_peak = jnp.max(scores, axis=3, keepdims=True)
    weights = jnp.exp(scores - row_peak)
    denominator = float(1 << level_index) * jnp.sum(weights, axis=3)
    numerator = jnp.einsum(
        "nhqk,nkhd->nqhd",
        weights.astype(jnp.bfloat16),
        value_blocks,
        preferred_element_type=jnp.float32,
    )
    block_count = query_blocks.shape[0]
    row_count = query_blocks.shape[1]
    peak_rows = jnp.transpose(row_peak[..., 0], (0, 2, 1)).reshape(block_count * row_count, -1)
    denominator_rows = jnp.transpose(denominator, (0, 2, 1)).reshape(block_count * row_count, -1)
    numerator_rows = numerator.reshape(
        block_count * row_count, numerator.shape[2], numerator.shape[3]
    )
    return (peak_rows, numerator_rows, denominator_rows)


def upper_half(device_index, bit):
    return device_index // (1 << bit) % 2 == 1


def assemble_one(piece, bit_count, device_index):
    for bit in range(bit_count):
        partner = partner_2(piece, "seq", bit)
        piece = jnp.where(
            upper_half(device_index, bit),
            jnp.concatenate([partner, piece], axis=1),
            jnp.concatenate([piece, partner], axis=1),
        )
    return piece


MESH = pl.DeviceIdType.MESH
NEG = -1e30
KERNEL_TOP = 4


def spread(level):
    return 1 << (level - 2)


def layer_kernel(seq_count, levels, extra, *refs):
    q_hbm, kv_hbm, w_hbm = refs[:3]
    refs = refs[3:]
    if extra:
        xm_ref, xn_ref, xr_ref = refs[:3]
        refs = refs[3:]
    out_ref = refs[0]
    q0, kv0, w, own, qc, far, att, peak, num, den, tm, tn, tr, psend, precv = refs[1:16]
    load_sem, send_sem, recv_sem, psend_sem, precv_sem = refs[16:]
    tokens, width = q_hbm.shape
    heads = width // BLOCK
    blocks = tokens // BLOCK
    half = out_ref.shape[1]
    scale = float(BLOCK) ** (-0.5)
    s = lax.axis_index("seq")
    h = lax.axis_index("head")
    other = 1 - h

    row_count = [tokens >> level for level in range(levels + 1)]
    start_row = [sum(row_count[1:level]) for level in range(levels + 1)]
    term_row = [sum(row_count[:level]) for level in range(levels + 1)]

    load_kv = pltpu.make_async_copy(kv_hbm, kv0.at[pl.ds(BLOCK, tokens)], load_sem.at[0])
    load_q = pltpu.make_async_copy(q_hbm, q0, load_sem.at[1])
    load_w = pltpu.make_async_copy(w_hbm, w, load_sem.at[2])
    load_kv.start()
    load_q.start()
    load_w.start()

    sends = {level: [] for level in range(levels + 1)}
    arrivals = {level: [] for level in range(levels + 1)}
    greet = []
    left_ok, right_ok = s >= 1, s + 1 < seq_count
    greet += [(left_ok, s - 1), (right_ok, s + 1)]
    sends[0] += [
        (right_ok, s + 1, kv_hbm.at[pl.ds(tokens - BLOCK, BLOCK)], kv0.at[pl.ds(0, BLOCK)], 0, 0),
        (left_ok, s - 1, kv_hbm.at[pl.ds(0, BLOCK)], kv0.at[pl.ds(BLOCK + tokens, BLOCK)], 1, 1),
    ]
    arrivals[0] += [(left_ok, sends[0][0][3], 0), (right_ok, sends[0][1][3], 1)]
    n1 = row_count[1]
    mine = own.at[pl.ds(0, n1)]
    sends[1] += [
        (right_ok, s + 1, mine, far.at[pl.ds(0, n1)], 2, 2),
        (left_ok, s - 1, mine, far.at[pl.ds(n1, n1)], 3, 3),
    ]
    arrivals[1] += [(left_ok, sends[1][0][3], 2), (right_ok, sends[1][1][3], 3)]
    sem = 4
    far_row = {1: 0}
    base = 2 * n1
    slot_ok = {}
    for level in range(2, levels + 1):
        far_row[level] = base
        group = spread(level)
        rows = row_count[level]
        block, place = s // group, s % group
        odd = block % 2
        total = seq_count // group
        mine = own.at[pl.ds(start_row[level], rows)]
        third = block + 3 - 6 * odd
        sources = [block - 2, block + 2, third]
        targets = [block + 2, block - 2, third]
        oks = []
        for slot in range(3):
            to_ok = (targets[slot] >= 0) & (targets[slot] < total)
            from_ok = (sources[slot] >= 0) & (sources[slot] < total)
            oks.append(from_ok)
            for peer in range(group):
                device = targets[slot] * group + peer
                landing = pl.multiple_of(base + slot * BLOCK + place * rows, rows)
                sends[level].append(
                    (to_ok, device, mine, far.at[pl.ds(landing, rows)], sem + slot * group + peer, sem + slot * group + place)
                )
                arrivals[level].append(
                    (from_ok, far.at[pl.ds(base + slot * BLOCK + peer * rows, rows)], sem + slot * group + peer)
                )
                greet.append((to_ok, device))
        slot_ok[level] = oks
        sem += 3 * group
        base += 3 * BLOCK

    barrier = pltpu.get_barrier_semaphore()
    pl.semaphore_signal(barrier, inc=1, device_id={"head": other}, device_id_type=MESH)
    greeted = jnp.int32(1)
    for ok, device in greet:
        @pl.when(ok)
        def _(device=device):
            pl.semaphore_signal(barrier, inc=1, device_id={"seq": device}, device_id_type=MESH)

        greeted = greeted + jnp.where(ok, 1, 0).astype(jnp.int32)
    pl.semaphore_wait(barrier, greeted)

    def copy_of(entry):
        ok, device, source, landing, out_sem, in_sem = entry
        return pltpu.make_async_remote_copy(
            src_ref=source, dst_ref=landing, send_sem=send_sem.at[out_sem], recv_sem=recv_sem.at[in_sem],
            device_id={"seq": device}, device_id_type=MESH,
        )

    def start_level(level):
        for entry in sends[level]:
            @pl.when(entry[0])
            def _(entry=entry):
                copy_of(entry).start()

    def wait_level(level):
        for ok, landing, in_sem in arrivals[level]:
            @pl.when(ok)
            def _(landing=landing, in_sem=in_sem):
                pltpu.make_async_remote_copy(
                    src_ref=landing, dst_ref=landing, send_sem=send_sem.at[in_sem], recv_sem=recv_sem.at[in_sem],
                    device_id={"seq": (s + 1) % seq_count}, device_id_type=MESH,
                ).wait_recv()

            @pl.when(jnp.logical_not(ok))
            def _(landing=landing):
                landing[...] = jnp.zeros(landing.shape, landing.dtype)

    start_level(0)

    chunk = 16 << levels
    load_kv.wait()

    def average(level):
        rows = chunk >> level
        position = lax.broadcasted_iota(jnp.int32, (rows, chunk), 1) >> level
        match = position == lax.broadcasted_iota(jnp.int32, (rows, chunk), 0)
        return jnp.where(match, 1.0 / (1 << level), 0.0).astype(jnp.bfloat16)

    for level in [1] + list(range(levels, 1, -1)):
        rows = chunk >> level
        matrix = average(level)
        for c in range(tokens // chunk):
            at = pl.ds(start_row[level] + c * rows, rows)
            tokens_at = pl.ds(BLOCK + c * chunk, chunk)
            own[at, 0:width] = jnp.dot(
                matrix, kv0[tokens_at, 0:width], preferred_element_type=jnp.float32
            ).astype(jnp.bfloat16)
            own[at, width : 2 * width] = (
                jnp.dot(matrix, kv0[tokens_at, width : 2 * width], preferred_element_type=jnp.float32)
                * float(1 << level)
            ).astype(jnp.bfloat16)
        start_level(level)
    load_q.wait()
    for level in range(1, levels + 1):
        rows = chunk >> level
        matrix = average(level)
        for c in range(tokens // chunk):
            qc[pl.ds(start_row[level] + c * rows, rows), :] = jnp.dot(
                matrix, q0[pl.ds(c * chunk, chunk), :], preferred_element_type=jnp.float32
            ).astype(jnp.bfloat16)

    def bias_of(oks):
        column = lax.broadcasted_iota(jnp.int32, (1, 3 * BLOCK), 1)
        b = [jnp.where(ok, 0.0, NEG).astype(jnp.float32) for ok in oks]
        return jnp.where(column < BLOCK, b[0], jnp.where(column < 2 * BLOCK, b[1], b[2]))

    def attend(level, q_ref, q_row, rows, kv_ref, pieces, bias, to_row):
        def one_head(head):
            cols = pl.ds(head * BLOCK, BLOCK)
            vcols = pl.ds(width + head * BLOCK, BLOCK)
            keys = jnp.concatenate([kv_ref[pl.ds(a, n), cols] for a, n in pieces], axis=0)
            values = jnp.concatenate([kv_ref[pl.ds(a, n), vcols] for a, n in pieces], axis=0)
            scores = lax.dot_general(
                q_ref[pl.ds(q_row, rows), cols], keys, (((1,), (1,)), ((), ())), preferred_element_type=jnp.float32
            ) * scale
            if bias is not None:
                scores = scores + bias
            top = jnp.max(scores, axis=1, keepdims=True)
            weights = jnp.exp(scores - top)
            sums = jnp.sum(weights, axis=1, keepdims=True) * float(1 << level)
            at = pl.ds(to_row, rows)
            num[at, cols] = jnp.dot(weights.astype(jnp.bfloat16), values, preferred_element_type=jnp.float32)
            peak[at, cols] = jnp.broadcast_to(top, (rows, BLOCK))
            den[at, cols] = jnp.broadcast_to(sums, (rows, BLOCK))

        for head in range(heads):
            one_head(head)

    yes = s >= 0
    for i in range(1, blocks - 1):
        attend(0, q0, i * BLOCK, BLOCK, kv0, [(i * BLOCK, 3 * BLOCK)], None, i * BLOCK)
    wait_level(0)
    last = blocks - 1
    attend(0, q0, 0, BLOCK, kv0, [(0, 3 * BLOCK)], bias_of([left_ok, yes, yes]), 0)
    attend(
        0, q0, last * BLOCK, BLOCK, kv0, [(last * BLOCK, 3 * BLOCK)], bias_of([yes, yes, right_ok]), last * BLOCK
    )
    wait_level(1)
    attend(
        1, qc, 0, BLOCK, far, [(0, BLOCK), (n1, n1)], bias_of([left_ok, right_ok, right_ok]), term_row[1]
    )
    attend(
        1, qc, BLOCK, BLOCK, far, [(0, n1), (n1 + BLOCK, BLOCK)], bias_of([left_ok, left_ok, right_ok]),
        term_row[1] + BLOCK,
    )
    for level in range(2, levels + 1):
        wait_level(level)
        attend(
            level, qc, start_row[level], row_count[level], far, [(far_row[level], 3 * BLOCK)],
            bias_of(slot_ok[level]), term_row[level],
        )

    for head in range(heads):
        cols = pl.ds(head * BLOCK, BLOCK)

        def terms(level):
            at = pl.ds(term_row[level], row_count[level])
            return peak[at, cols], num[at, cols], den[at, cols]

        def merge(a, b):
            m = jnp.maximum(a[0], b[0])
            fa, fb = jnp.exp(a[0] - m), jnp.exp(b[0] - m)
            return m, fa * a[1] + fb * b[1], fa * a[2] + fb * b[2]

        state = terms(levels)
        if extra:
            state = merge(state, (xm_ref[:, cols], xn_ref[:, cols], xr_ref[:, cols]))
        for level in range(levels - 1, -1, -1):
            n = row_count[level + 1]
            for ref, value in zip((tm, tn, tr), state):
                ref[pl.ds(0, n, 2), :] = value
                ref[pl.ds(1, n, 2), :] = value
            wide = tuple(ref[pl.ds(0, 2 * n), :] for ref in (tm, tn, tr))
            state = merge(wide, terms(level))
        att[:, cols] = (state[1] / state[2]).astype(jnp.bfloat16)

    load_w.wait()
    theirs = pl.ds(pl.multiple_of(other * half, BLOCK), half)
    ours = pl.ds(pl.multiple_of(h * half, BLOCK), half)

    def share(c):
        at = pl.ds(c * BLOCK, BLOCK)
        return pltpu.make_async_remote_copy(
            src_ref=psend.at[at], dst_ref=precv.at[at], send_sem=psend_sem.at[c], recv_sem=precv_sem.at[c],
            device_id={"head": other}, device_id_type=MESH,
        )

    for c in range(blocks):
        at = pl.ds(c * BLOCK, BLOCK)
        psend[at, :] = jnp.dot(att[at, :], w[:, theirs], preferred_element_type=jnp.float32).astype(jnp.bfloat16)
        share(c).start()
    for c in range(blocks):
        at = pl.ds(c * BLOCK, BLOCK)
        kept = jnp.dot(att[at, :], w[:, ours], preferred_element_type=jnp.float32).astype(jnp.bfloat16)
        share(c).wait_recv()
        out_ref[at, :] = (kept.astype(jnp.float32) + precv[at, :].astype(jnp.float32)).astype(jnp.bfloat16)
    for c in range(blocks):
        share(c).wait_send()
    for level in range(levels + 1):
        for entry in sends[level]:
            @pl.when(entry[0])
            def _(entry=entry):
                copy_of(entry).wait_send()


def upper_terms(query_rows, key_rows, value_rows, first, top, rows_at):
    seq_count = lax.axis_size("seq")
    device_index = lax.axis_index("seq")
    scale = float(query_rows.shape[2]) ** (-0.5)
    merged = None
    for level_index in range(first, top + 1):
        queries = coarsen(query_rows, level_index, True)
        piece = jnp.stack([coarsen(key_rows, level_index, True), coarsen(value_rows, level_index, False)])
        whole_block = assemble_one(piece, level_index - 2, device_index)
        group = 1 << level_index - 2
        before_two = shifted(whole_block, "seq", 2 * group)
        after_two = shifted(whole_block, "seq", -2 * group)
        block_index = device_index // group
        outgoing = jnp.where(block_index % 2 == 0, before_two, after_two)
        third_block = partner_2(outgoing, "seq", level_index - 2)
        level_keys = jnp.concatenate([before_two, after_two, third_block], axis=1)[:, None]
        valid = slot_masks(jnp.reshape(block_index, (1,)), seq_count // group, level_index, BLOCK)
        terms = level_attend(queries[None], level_keys[0], level_keys[1], valid, level_index, scale)
        terms = [jnp.repeat(term, rows_at // term.shape[0], axis=0) for term in terms]
        if merged is None:
            merged = terms
        else:
            m = jnp.maximum(merged[0], terms[0])
            fa, fb = jnp.exp(merged[0] - m), jnp.exp(terms[0] - m)
            merged = [
                m,
                fa[:, :, None] * merged[1] + fb[:, :, None] * terms[1],
                fa * merged[2] + fb * terms[2],
            ]
    flat = (rows_at, merged[1].shape[1] * merged[1].shape[2])
    wide = [jnp.broadcast_to(x[:, :, None], merged[1].shape).reshape(flat) for x in (merged[0], merged[2])]
    return [wide[0], merged[1].reshape(flat), wide[1]]


def per_device(query_rows, key_rows, value_rows, out_weight):
    seq_count = lax.axis_size("seq")
    tokens, heads, head_size = query_rows.shape
    width = heads * head_size
    features = out_weight.shape[2]
    half = features // lax.axis_size("head")
    top = seq_count.bit_length() - 1
    levels = min(top, KERNEL_TOP)
    extra = []
    if top > levels:
        extra = upper_terms(query_rows, key_rows, value_rows, levels + 1, top, tokens >> levels)
    queries = query_rows.reshape(tokens, width)
    pairs = jnp.concatenate([key_rows.reshape(tokens, width), value_rows.reshape(tokens, width)], axis=1)
    weight = out_weight.reshape(width, features)
    coarse = sum(tokens >> level for level in range(1, levels + 1))
    far_rows = 2 * (tokens >> 1) + 3 * BLOCK * (levels - 1)
    copies = 4 + sum(3 * spread(level) for level in range(2, levels + 1))
    blocks = tokens // BLOCK
    bf16, f32 = jnp.bfloat16, jnp.float32
    return pl.pallas_call(
        functools.partial(layer_kernel, seq_count, levels, bool(extra)),
        out_shape=jax.ShapeDtypeStruct((tokens, half), bf16),
        in_specs=[pl.BlockSpec(memory_space=pl.ANY)] * 3 + [pl.BlockSpec(memory_space=pltpu.VMEM)] * len(extra),
        out_specs=pl.BlockSpec(memory_space=pltpu.VMEM),
        scratch_shapes=[
            pltpu.VMEM((tokens, width), bf16),
            pltpu.VMEM((tokens + 2 * BLOCK, 2 * width), bf16),
            pltpu.VMEM((width, features), bf16),
            pltpu.VMEM((coarse, 2 * width), bf16),
            pltpu.VMEM((coarse, width), bf16),
            pltpu.VMEM((far_rows, 2 * width), bf16),
            pltpu.VMEM((tokens, width), bf16),
            pltpu.VMEM((tokens + coarse, width), f32),
            pltpu.VMEM((tokens + coarse, width), f32),
            pltpu.VMEM((tokens + coarse, width), f32),
            pltpu.VMEM((tokens, BLOCK), f32),
            pltpu.VMEM((tokens, BLOCK), f32),
            pltpu.VMEM((tokens, BLOCK), f32),
            pltpu.VMEM((tokens, half), bf16),
            pltpu.VMEM((tokens, half), bf16),
            pltpu.SemaphoreType.DMA((3,)),
            pltpu.SemaphoreType.DMA((copies,)),
            pltpu.SemaphoreType.DMA((copies,)),
            pltpu.SemaphoreType.DMA((blocks,)),
            pltpu.SemaphoreType.DMA((blocks,)),
        ],
        compiler_params=pltpu.CompilerParams(
            collective_id=0, has_side_effects=True, vmem_limit_bytes=48 * 2**20
        ),
        cost_estimate=pl.CostEstimate(flops=3 * 10**9, bytes_accessed=6 * 2**20, transcendentals=2 * 10**6),
    )(queries, pairs, weight, *extra)


def solution(mesh):
    return jax.shard_map(
        per_device,
        mesh=mesh,
        in_specs=(
            P("seq", "head", None),
            P("seq", "head", None),
            P("seq", "head", None),
            P("head", None, None),
        ),
        out_specs=P("seq", "head"),
        check_vma=False,
    )
```

```python
import functools

import jax
import jax.numpy as jnp
from jax import lax
from jax.experimental import pallas as pl
from jax.experimental.pallas import tpu as pltpu
from jax.sharding import PartitionSpec as P

BLOCK = 128


def partner_2(value, axis, distance):
    mask = 2**distance
    pairs = [(source, source ^ mask) for source in range(lax.axis_size(axis))]
    return lax.ppermute(value, axis, pairs)


def shifted(value, axis, steps):
    count = lax.axis_size(axis)
    initial, last = (max(0, -steps), min(count, count - steps))
    return lax.ppermute(value, axis, [(source, source + steps) for source in range(initial, last)])


def coarsen(source, level_index, average):
    count = source.shape[0] >> level_index
    grouped = source.astype(jnp.float32).reshape((count, 1 << level_index) + source.shape[1:])
    summed = jnp.sum(grouped, axis=1)
    if average:
        summed = summed / float(1 << level_index)
    return summed.astype(jnp.bfloat16)


def slot_targets(block_index, level_index):
    if level_index == 0:
        return [block_index - 1, block_index, block_index + 1]
    return [
        block_index - 2,
        block_index + 2,
        jnp.where(block_index % 2 == 0, block_index + 3, block_index - 3),
    ]


def slot_masks(block_index, block_total, level_index, width):
    targets = slot_targets(block_index, level_index)
    return jnp.concatenate(
        [
            jnp.repeat(((target >= 0) & (target < block_total))[:, None], width, axis=1)
            for target in targets
        ],
        axis=1,
    )


def level_attend(query_blocks, key_blocks, value_blocks, valid, level_index, scale):
    scores = (
        jnp.einsum("nqhd,nkhd->nhqk", query_blocks, key_blocks, preferred_element_type=jnp.float32)
        * scale
    )
    scores = jnp.where(valid[:, None, None, :], scores, -jnp.inf)
    row_peak = jnp.max(scores, axis=3, keepdims=True)
    weights = jnp.exp(scores - row_peak)
    denominator = float(1 << level_index) * jnp.sum(weights, axis=3)
    numerator = jnp.einsum(
        "nhqk,nkhd->nqhd",
        weights.astype(jnp.bfloat16),
        value_blocks,
        preferred_element_type=jnp.float32,
    )
    block_count = query_blocks.shape[0]
    row_count = query_blocks.shape[1]
    peak_rows = jnp.transpose(row_peak[..., 0], (0, 2, 1)).reshape(block_count * row_count, -1)
    denominator_rows = jnp.transpose(denominator, (0, 2, 1)).reshape(block_count * row_count, -1)
    numerator_rows = numerator.reshape(
        block_count * row_count, numerator.shape[2], numerator.shape[3]
    )
    return (peak_rows, numerator_rows, denominator_rows)


def upper_half(device_index, bit):
    return device_index // (1 << bit) % 2 == 1


def assemble_one(piece, bit_count, device_index):
    for bit in range(bit_count):
        partner = partner_2(piece, "seq", bit)
        piece = jnp.where(
            upper_half(device_index, bit),
            jnp.concatenate([partner, piece], axis=1),
            jnp.concatenate([piece, partner], axis=1),
        )
    return piece


MESH = pl.DeviceIdType.MESH
NEG = -1e30
KERNEL_TOP = 4


def spread(level):
    return 1 << (level - 2)


def layer_kernel(seq_count, levels, extra, *refs):
    q_hbm, kv_hbm, w_hbm = refs[:3]
    refs = refs[3:]
    if extra:
        xm_ref, xn_ref, xr_ref = refs[:3]
        refs = refs[3:]
    out_ref = refs[0]
    q0, kv0, w, own, qc, far, att, peak, num, den, tm, tn, tr, psend, precv = refs[1:16]
    load_sem, send_sem, recv_sem, psend_sem, precv_sem = refs[16:]
    tokens, width = q_hbm.shape
    heads = width // BLOCK
    blocks = tokens // BLOCK
    half = out_ref.shape[1]
    scale = float(BLOCK) ** (-0.5)
    s = lax.axis_index("seq")
    h = lax.axis_index("head")
    other = 1 - h

    row_count = [tokens >> level for level in range(levels + 1)]
    start_row = [sum(row_count[1:level]) for level in range(levels + 1)]
    term_row = [sum(row_count[:level]) for level in range(levels + 1)]

    load_kv = pltpu.make_async_copy(kv_hbm, kv0.at[pl.ds(BLOCK, tokens)], load_sem.at[0])
    load_q = pltpu.make_async_copy(q_hbm, q0, load_sem.at[1])
    load_w = pltpu.make_async_copy(w_hbm, w, load_sem.at[2])
    load_kv.start()
    load_q.start()
    load_w.start()

    sends = {level: [] for level in range(levels + 1)}
    arrivals = {level: [] for level in range(levels + 1)}
    greet = []
    left_ok, right_ok = s >= 1, s + 1 < seq_count
    greet += [(left_ok, s - 1), (right_ok, s + 1)]
    sends[0] += [
        (right_ok, s + 1, kv_hbm.at[pl.ds(tokens - BLOCK, BLOCK)], kv0.at[pl.ds(0, BLOCK)], 0, 0),
        (left_ok, s - 1, kv_hbm.at[pl.ds(0, BLOCK)], kv0.at[pl.ds(BLOCK + tokens, BLOCK)], 1, 1),
    ]
    arrivals[0] += [(left_ok, sends[0][0][3], 0), (right_ok, sends[0][1][3], 1)]
    n1 = row_count[1]
    edge = BLOCK // 2
    sends[1] += [
        (right_ok, s + 1, own.at[pl.ds(0, n1 - edge)], far.at[pl.ds(0, n1 - edge)], 2, 2),
        (left_ok, s - 1, own.at[pl.ds(edge, n1 - edge)], far.at[pl.ds(n1 + edge, n1 - edge)], 3, 3),
    ]
    arrivals[1] += [(left_ok, sends[1][0][3], 2), (right_ok, sends[1][1][3], 3)]
    sem = 4
    far_row = {1: 0}
    own_row = {1: 0}
    gathers = {level: [] for level in range(2, levels + 1)}
    gathered = {level: [] for level in range(2, levels + 1)}
    base = 2 * n1
    slot_ok = {}
    for level in range(2, levels + 1):
        far_row[level] = base
        group = spread(level)
        rows = row_count[level]
        block, place = s // group, s % group
        odd = block % 2
        total = seq_count // group
        own_row[level] = n1 + (level - 2) * BLOCK
        third = block + 3 - 6 * odd
        sources = [block - 2, block + 2, third]
        targets = [block + 2, block - 2, third]

        def piece(at, level=level, rows=rows):
            return own.at[pl.ds(pl.multiple_of(own_row[level] + at * rows, rows), rows)]

        for step in range(1, group):
            device = block * group + (place + step) % group
            gathers[level].append((s >= 0, device, piece(place), piece(place), sem, sem))
            gathered[level].append((s >= 0, piece((place + group - step) % group), sem))
            greet.append((s >= 0, device))
            sem += 1
        oks = []
        whole = own.at[pl.ds(own_row[level], BLOCK)]
        for slot in range(3):
            to_ok = (targets[slot] >= 0) & (targets[slot] < total)
            from_ok = (sources[slot] >= 0) & (sources[slot] < total)
            oks.append(from_ok)
            landing = far.at[pl.ds(base + slot * BLOCK, BLOCK)]
            device = targets[slot] * group + place
            sends[level].append((to_ok, device, whole, landing, sem, sem))
            arrivals[level].append((from_ok, landing, sem))
            greet.append((to_ok, device))
            sem += 1
        slot_ok[level] = oks
        base += 3 * BLOCK

    barrier = pltpu.get_barrier_semaphore()
    pl.semaphore_signal(barrier, inc=1, device_id={"head": other}, device_id_type=MESH)
    greeted = jnp.int32(1)
    for ok, device in greet:
        @pl.when(ok)
        def _(device=device):
            pl.semaphore_signal(barrier, inc=1, device_id={"seq": device}, device_id_type=MESH)

        greeted = greeted + jnp.where(ok, 1, 0).astype(jnp.int32)
    pl.semaphore_wait(barrier, greeted)

    def copy_of(entry):
        ok, device, source, landing, out_sem, in_sem = entry
        return pltpu.make_async_remote_copy(
            src_ref=source, dst_ref=landing, send_sem=send_sem.at[out_sem], recv_sem=recv_sem.at[in_sem],
            device_id={"seq": device}, device_id_type=MESH,
        )

    def start_all(entries):
        for entry in entries:
            @pl.when(entry[0])
            def _(entry=entry):
                copy_of(entry).start()

    def start_whole(level):
        for ok, landing, in_sem in gathered[level]:
            pltpu.make_async_remote_copy(
                src_ref=landing, dst_ref=landing, send_sem=send_sem.at[in_sem], recv_sem=recv_sem.at[in_sem],
                device_id={"seq": (s + 1) % seq_count}, device_id_type=MESH,
            ).wait_recv()
        start_all(sends[level])

    def wait_level(level):
        for ok, landing, in_sem in arrivals[level]:
            @pl.when(ok)
            def _(landing=landing, in_sem=in_sem):
                pltpu.make_async_remote_copy(
                    src_ref=landing, dst_ref=landing, send_sem=send_sem.at[in_sem], recv_sem=recv_sem.at[in_sem],
                    device_id={"seq": (s + 1) % seq_count}, device_id_type=MESH,
                ).wait_recv()

            @pl.when(jnp.logical_not(ok))
            def _(landing=landing):
                landing[...] = jnp.zeros(landing.shape, landing.dtype)

    chunk = 16 << levels
    load_kv.wait()

    def average(level, chunk=chunk):
        rows = chunk >> level
        position = lax.broadcasted_iota(jnp.int32, (rows, chunk), 1) >> level
        match = position == lax.broadcasted_iota(jnp.int32, (rows, chunk), 0)
        return jnp.where(match, 1.0 / (1 << level), 0.0).astype(jnp.bfloat16)

    def shrink(level, matrix, kv_row, count, to_ref, to_row):
        tokens_at, at = pl.ds(kv_row, count), pl.ds(to_row, count >> level)
        to_ref[at, 0:width] = jnp.dot(
            matrix, kv0[tokens_at, 0:width], preferred_element_type=jnp.float32
        ).astype(jnp.bfloat16)
        to_ref[at, width : 2 * width] = (
            jnp.dot(matrix, kv0[tokens_at, width : 2 * width], preferred_element_type=jnp.float32)
            * float(1 << level)
        ).astype(jnp.bfloat16)

    for level in range(levels, 0, -1):
        rows = chunk >> level
        matrix = average(level)
        place = s % spread(level) if level > 1 else 0
        for c in range(tokens // chunk):
            to_row = own_row[level] + place * row_count[level] + c * rows
            if level > 1:
                to_row = pl.multiple_of(to_row, rows)
            shrink(level, matrix, BLOCK + c * chunk, chunk, own, to_row)
        if level > 2:
            start_all(gathers[level])
            if level == 3:
                start_all(sends[0])
        else:
            start_all(sends[level])
    load_q.wait()
    for level in range(1, levels + 1):
        rows = chunk >> level
        matrix = average(level)
        for c in range(tokens // chunk):
            qc[pl.ds(start_row[level] + c * rows, rows), :] = jnp.dot(
                matrix, q0[pl.ds(c * chunk, chunk), :], preferred_element_type=jnp.float32
            ).astype(jnp.bfloat16)

    def bias_of(oks):
        column = lax.broadcasted_iota(jnp.int32, (1, 3 * BLOCK), 1)
        b = [jnp.where(ok, 0.0, NEG).astype(jnp.float32) for ok in oks]
        return jnp.where(column < BLOCK, b[0], jnp.where(column < 2 * BLOCK, b[1], b[2]))

    def attend(level, q_ref, q_row, rows, kv_ref, pieces, bias, to_row):
        def one_head(head):
            cols = pl.ds(head * BLOCK, BLOCK)
            vcols = pl.ds(width + head * BLOCK, BLOCK)
            keys = jnp.concatenate([kv_ref[pl.ds(a, n), cols] for a, n in pieces], axis=0)
            values = jnp.concatenate([kv_ref[pl.ds(a, n), vcols] for a, n in pieces], axis=0)
            scores = lax.dot_general(
                q_ref[pl.ds(q_row, rows), cols], keys, (((1,), (1,)), ((), ())), preferred_element_type=jnp.float32
            ) * scale
            if bias is not None:
                scores = scores + bias
            top = jnp.max(scores, axis=1, keepdims=True)
            weights = jnp.exp(scores - top)
            sums = jnp.sum(weights, axis=1, keepdims=True) * float(1 << level)
            at = pl.ds(to_row, rows)
            num[at, cols] = jnp.dot(weights.astype(jnp.bfloat16), values, preferred_element_type=jnp.float32)
            peak[at, cols] = jnp.broadcast_to(top, (rows, BLOCK))
            den[at, cols] = jnp.broadcast_to(sums, (rows, BLOCK))

        for head in range(heads):
            one_head(head)

    yes = s >= 0
    for i in range(1, blocks - 1):
        attend(0, q0, i * BLOCK, BLOCK, kv0, [(i * BLOCK, 3 * BLOCK)], None, i * BLOCK)
    for level in range(levels, 2, -1):
        start_whole(level)
    wait_level(0)
    last = blocks - 1
    attend(0, q0, 0, BLOCK, kv0, [(0, 3 * BLOCK)], bias_of([left_ok, yes, yes]), 0)
    attend(
        0, q0, last * BLOCK, BLOCK, kv0, [(last * BLOCK, 3 * BLOCK)], bias_of([yes, yes, right_ok]), last * BLOCK
    )
    wait_level(1)
    matrix = average(1, BLOCK)
    shrink(1, matrix, 0, BLOCK, far, n1 - edge)
    shrink(1, matrix, BLOCK + tokens, BLOCK, far, n1)
    attend(
        1, qc, 0, BLOCK, far, [(0, BLOCK), (n1, n1)], bias_of([left_ok, right_ok, right_ok]), term_row[1]
    )
    attend(
        1, qc, BLOCK, BLOCK, far, [(0, n1), (n1 + BLOCK, BLOCK)], bias_of([left_ok, left_ok, right_ok]),
        term_row[1] + BLOCK,
    )
    for level in range(2, levels + 1):
        wait_level(level)
        attend(
            level, qc, start_row[level], row_count[level], far, [(far_row[level], 3 * BLOCK)],
            bias_of(slot_ok[level]), term_row[level],
        )

    for head in range(heads):
        cols = pl.ds(head * BLOCK, BLOCK)

        def terms(level):
            at = pl.ds(term_row[level], row_count[level])
            return peak[at, cols], num[at, cols], den[at, cols]

        def merge(a, b):
            m = jnp.maximum(a[0], b[0])
            fa, fb = jnp.exp(a[0] - m), jnp.exp(b[0] - m)
            return m, fa * a[1] + fb * b[1], fa * a[2] + fb * b[2]

        state = terms(levels)
        if extra:
            state = merge(state, (xm_ref[:, cols], xn_ref[:, cols], xr_ref[:, cols]))
        for level in range(levels - 1, -1, -1):
            n = row_count[level + 1]
            for ref, value in zip((tm, tn, tr), state):
                ref[pl.ds(0, n, 2), :] = value
                ref[pl.ds(1, n, 2), :] = value
            wide = tuple(ref[pl.ds(0, 2 * n), :] for ref in (tm, tn, tr))
            state = merge(wide, terms(level))
        att[:, cols] = (state[1] / state[2]).astype(jnp.bfloat16)

    load_w.wait()
    theirs = pl.ds(pl.multiple_of(other * half, BLOCK), half)
    ours = pl.ds(pl.multiple_of(h * half, BLOCK), half)

    def share(c):
        at = pl.ds(c * BLOCK, BLOCK)
        return pltpu.make_async_remote_copy(
            src_ref=psend.at[at], dst_ref=precv.at[at], send_sem=psend_sem.at[c], recv_sem=precv_sem.at[c],
            device_id={"head": other}, device_id_type=MESH,
        )

    for c in range(blocks):
        at = pl.ds(c * BLOCK, BLOCK)
        psend[at, :] = jnp.dot(att[at, :], w[:, theirs], preferred_element_type=jnp.float32).astype(jnp.bfloat16)
        share(c).start()
    for c in range(blocks):
        at = pl.ds(c * BLOCK, BLOCK)
        kept = jnp.dot(att[at, :], w[:, ours], preferred_element_type=jnp.float32).astype(jnp.bfloat16)
        share(c).wait_recv()
        out_ref[at, :] = (kept.astype(jnp.float32) + precv[at, :].astype(jnp.float32)).astype(jnp.bfloat16)
    for c in range(blocks):
        share(c).wait_send()
    for level in range(levels + 1):
        for entry in gathers.get(level, []) + sends[level]:
            @pl.when(entry[0])
            def _(entry=entry):
                copy_of(entry).wait_send()


def upper_terms(query_rows, key_rows, value_rows, first, top, rows_at):
    seq_count = lax.axis_size("seq")
    device_index = lax.axis_index("seq")
    scale = float(query_rows.shape[2]) ** (-0.5)
    merged = None
    for level_index in range(first, top + 1):
        queries = coarsen(query_rows, level_index, True)
        piece = jnp.stack([coarsen(key_rows, level_index, True), coarsen(value_rows, level_index, False)])
        whole_block = assemble_one(piece, level_index - 2, device_index)
        group = 1 << level_index - 2
        before_two = shifted(whole_block, "seq", 2 * group)
        after_two = shifted(whole_block, "seq", -2 * group)
        block_index = device_index // group
        outgoing = jnp.where(block_index % 2 == 0, before_two, after_two)
        third_block = partner_2(outgoing, "seq", level_index - 2)
        level_keys = jnp.concatenate([before_two, after_two, third_block], axis=1)[:, None]
        valid = slot_masks(jnp.reshape(block_index, (1,)), seq_count // group, level_index, BLOCK)
        terms = level_attend(queries[None], level_keys[0], level_keys[1], valid, level_index, scale)
        terms = [jnp.repeat(term, rows_at // term.shape[0], axis=0) for term in terms]
        if merged is None:
            merged = terms
        else:
            m = jnp.maximum(merged[0], terms[0])
            fa, fb = jnp.exp(merged[0] - m), jnp.exp(terms[0] - m)
            merged = [
                m,
                fa[:, :, None] * merged[1] + fb[:, :, None] * terms[1],
                fa * merged[2] + fb * terms[2],
            ]
    flat = (rows_at, merged[1].shape[1] * merged[1].shape[2])
    wide = [jnp.broadcast_to(x[:, :, None], merged[1].shape).reshape(flat) for x in (merged[0], merged[2])]
    return [wide[0], merged[1].reshape(flat), wide[1]]


def per_device(query_rows, key_rows, value_rows, out_weight):
    seq_count = lax.axis_size("seq")
    tokens, heads, head_size = query_rows.shape
    width = heads * head_size
    features = out_weight.shape[2]
    half = features // lax.axis_size("head")
    top = seq_count.bit_length() - 1
    levels = min(top, KERNEL_TOP)
    extra = []
    if top > levels:
        extra = upper_terms(query_rows, key_rows, value_rows, levels + 1, top, tokens >> levels)
    queries = query_rows.reshape(tokens, width)
    pairs = jnp.concatenate([key_rows.reshape(tokens, width), value_rows.reshape(tokens, width)], axis=1)
    weight = out_weight.reshape(width, features)
    coarse = sum(tokens >> level for level in range(1, levels + 1))
    far_rows = 2 * (tokens >> 1) + 3 * BLOCK * (levels - 1)
    copies = 4 + sum(2 + spread(level) for level in range(2, levels + 1))
    blocks = tokens // BLOCK
    bf16, f32 = jnp.bfloat16, jnp.float32
    return pl.pallas_call(
        functools.partial(layer_kernel, seq_count, levels, bool(extra)),
        out_shape=jax.ShapeDtypeStruct((tokens, half), bf16),
        in_specs=[pl.BlockSpec(memory_space=pl.ANY)] * 3 + [pl.BlockSpec(memory_space=pltpu.VMEM)] * len(extra),
        out_specs=pl.BlockSpec(memory_space=pltpu.VMEM),
        scratch_shapes=[
            pltpu.VMEM((tokens, width), bf16),
            pltpu.VMEM((tokens + 2 * BLOCK, 2 * width), bf16),
            pltpu.VMEM((width, features), bf16),
            pltpu.VMEM((tokens // 2 + BLOCK * (levels - 1), 2 * width), bf16),
            pltpu.VMEM((coarse, width), bf16),
            pltpu.VMEM((far_rows, 2 * width), bf16),
            pltpu.VMEM((tokens, width), bf16),
            pltpu.VMEM((tokens + coarse, width), f32),
            pltpu.VMEM((tokens + coarse, width), f32),
            pltpu.VMEM((tokens + coarse, width), f32),
            pltpu.VMEM((tokens, BLOCK), f32),
            pltpu.VMEM((tokens, BLOCK), f32),
            pltpu.VMEM((tokens, BLOCK), f32),
            pltpu.VMEM((tokens, half), bf16),
            pltpu.VMEM((tokens, half), bf16),
            pltpu.SemaphoreType.DMA((3,)),
            pltpu.SemaphoreType.DMA((copies,)),
            pltpu.SemaphoreType.DMA((copies,)),
            pltpu.SemaphoreType.DMA((blocks,)),
            pltpu.SemaphoreType.DMA((blocks,)),
        ],
        compiler_params=pltpu.CompilerParams(
            collective_id=0, has_side_effects=True, vmem_limit_bytes=48 * 2**20
        ),
        cost_estimate=pl.CostEstimate(flops=3 * 10**9, bytes_accessed=6 * 2**20, transcendentals=2 * 10**6),
    )(queries, pairs, weight, *extra)


def solution(mesh):
    return jax.shard_map(
        per_device,
        mesh=mesh,
        in_specs=(
            P("seq", "head", None),
            P("seq", "head", None),
            P("seq", "head", None),
            P("head", None, None),
        ),
        out_specs=P("seq", "head"),
        check_vma=False,
    )
```

```python
import functools

import jax
import jax.numpy as jnp
from jax import lax
from jax.experimental import pallas as pl
from jax.experimental.pallas import tpu as pltpu
from jax.sharding import PartitionSpec as P

BLOCK = 128


def partner_2(value, axis, distance):
    mask = 2**distance
    pairs = [(source, source ^ mask) for source in range(lax.axis_size(axis))]
    return lax.ppermute(value, axis, pairs)


def shifted(value, axis, steps):
    count = lax.axis_size(axis)
    initial, last = (max(0, -steps), min(count, count - steps))
    return lax.ppermute(value, axis, [(source, source + steps) for source in range(initial, last)])


def coarsen(source, level_index, average):
    count = source.shape[0] >> level_index
    grouped = source.astype(jnp.float32).reshape((count, 1 << level_index) + source.shape[1:])
    summed = jnp.sum(grouped, axis=1)
    if average:
        summed = summed / float(1 << level_index)
    return summed.astype(jnp.bfloat16)


def slot_targets(block_index, level_index):
    if level_index == 0:
        return [block_index - 1, block_index, block_index + 1]
    return [
        block_index - 2,
        block_index + 2,
        jnp.where(block_index % 2 == 0, block_index + 3, block_index - 3),
    ]


def slot_masks(block_index, block_total, level_index, width):
    targets = slot_targets(block_index, level_index)
    return jnp.concatenate(
        [
            jnp.repeat(((target >= 0) & (target < block_total))[:, None], width, axis=1)
            for target in targets
        ],
        axis=1,
    )


def level_attend(query_blocks, key_blocks, value_blocks, valid, level_index, scale):
    scores = (
        jnp.einsum("nqhd,nkhd->nhqk", query_blocks, key_blocks, preferred_element_type=jnp.float32)
        * scale
    )
    scores = jnp.where(valid[:, None, None, :], scores, -jnp.inf)
    row_peak = jnp.max(scores, axis=3, keepdims=True)
    weights = jnp.exp(scores - row_peak)
    denominator = float(1 << level_index) * jnp.sum(weights, axis=3)
    numerator = jnp.einsum(
        "nhqk,nkhd->nqhd",
        weights.astype(jnp.bfloat16),
        value_blocks,
        preferred_element_type=jnp.float32,
    )
    block_count = query_blocks.shape[0]
    row_count = query_blocks.shape[1]
    peak_rows = jnp.transpose(row_peak[..., 0], (0, 2, 1)).reshape(block_count * row_count, -1)
    denominator_rows = jnp.transpose(denominator, (0, 2, 1)).reshape(block_count * row_count, -1)
    numerator_rows = numerator.reshape(
        block_count * row_count, numerator.shape[2], numerator.shape[3]
    )
    return (peak_rows, numerator_rows, denominator_rows)


def upper_half(device_index, bit):
    return device_index // (1 << bit) % 2 == 1


def assemble_one(piece, bit_count, device_index):
    for bit in range(bit_count):
        partner = partner_2(piece, "seq", bit)
        piece = jnp.where(
            upper_half(device_index, bit),
            jnp.concatenate([partner, piece], axis=1),
            jnp.concatenate([piece, partner], axis=1),
        )
    return piece


MESH = pl.DeviceIdType.MESH
NEG = -1e30
KERNEL_TOP = 4


def spread(level):
    return 1 << (level - 2)


def layer_kernel(seq_count, levels, extra, *refs):
    q_hbm, kv_hbm, w_hbm = refs[:3]
    refs = refs[3:]
    if extra:
        xm_ref, xn_ref, xr_ref = refs[:3]
        refs = refs[3:]
    out_ref = refs[0]
    q0, kv0, w, own, qc, far, att, peak, num, den, tm, tn, tr, psend, precv = refs[1:16]
    load_sem, send_sem, recv_sem, psend_sem, precv_sem = refs[16:]
    tokens, width = q_hbm.shape
    heads = width // BLOCK
    blocks = tokens // BLOCK
    half = out_ref.shape[1]
    scale = float(BLOCK) ** (-0.5)
    s = lax.axis_index("seq")
    h = lax.axis_index("head")
    other = 1 - h

    row_count = [tokens >> level for level in range(levels + 1)]
    start_row = [sum(row_count[1:level]) for level in range(levels + 1)]
    term_row = [sum(row_count[:level]) for level in range(levels + 1)]

    load_kv = pltpu.make_async_copy(kv_hbm, kv0.at[pl.ds(BLOCK, tokens)], load_sem.at[0])
    load_q = pltpu.make_async_copy(q_hbm, q0, load_sem.at[1])
    load_w = pltpu.make_async_copy(w_hbm, w, load_sem.at[2])
    load_kv.start()
    load_q.start()
    load_w.start()

    sends = {level: [] for level in range(levels + 1)}
    arrivals = {level: [] for level in range(levels + 1)}
    greet = []
    left_ok, right_ok = s >= 1, s + 1 < seq_count
    greet += [(left_ok, s - 1), (right_ok, s + 1)]
    sends[0] += [
        (right_ok, s + 1, kv_hbm.at[pl.ds(tokens - BLOCK, BLOCK)], kv0.at[pl.ds(0, BLOCK)], 0, 0),
        (left_ok, s - 1, kv_hbm.at[pl.ds(0, BLOCK)], kv0.at[pl.ds(BLOCK + tokens, BLOCK)], 1, 1),
    ]
    arrivals[0] += [(left_ok, sends[0][0][3], 0), (right_ok, sends[0][1][3], 1)]
    n1 = row_count[1]
    edge = BLOCK // 2
    sends[1] += [
        (right_ok, s + 1, own.at[pl.ds(0, n1 - edge)], far.at[pl.ds(0, n1 - edge)], 2, 2),
        (left_ok, s - 1, own.at[pl.ds(edge, n1 - edge)], far.at[pl.ds(n1 + edge, n1 - edge)], 3, 3),
    ]
    arrivals[1] += [(left_ok, sends[1][0][3], 2), (right_ok, sends[1][1][3], 3)]
    sem = 4
    far_row = {1: 0}
    own_row = {1: 0}
    gathers = {level: [] for level in range(2, levels + 1)}
    gathered = {level: [] for level in range(2, levels + 1)}
    base = 2 * n1
    slot_ok = {}
    for level in range(2, levels + 1):
        far_row[level] = base
        group = spread(level)
        rows = row_count[level]
        block, place = s // group, s % group
        odd = block % 2
        total = seq_count // group
        own_row[level] = n1 + (level - 2) * BLOCK
        third = block + 3 - 6 * odd
        sources = [block - 2, block + 2, third]
        targets = [block + 2, block - 2, third]

        def piece(at, level=level, rows=rows):
            return own.at[pl.ds(pl.multiple_of(own_row[level] + at * rows, rows), rows)]

        for step in range(1, group):
            device = block * group + (place + step) % group
            gathers[level].append((s >= 0, device, piece(place), piece(place), sem, sem))
            gathered[level].append((s >= 0, piece((place + group - step) % group), sem))
            greet.append((s >= 0, device))
            sem += 1
        oks = []
        whole = own.at[pl.ds(own_row[level], BLOCK)]
        for slot in range(3):
            to_ok = (targets[slot] >= 0) & (targets[slot] < total)
            from_ok = (sources[slot] >= 0) & (sources[slot] < total)
            oks.append(from_ok)
            landing = far.at[pl.ds(base + slot * BLOCK, BLOCK)]
            device = targets[slot] * group + place
            sends[level].append((to_ok, device, whole, landing, sem, sem))
            arrivals[level].append((from_ok, landing, sem))
            greet.append((to_ok, device))
            sem += 1
        slot_ok[level] = oks
        base += 3 * BLOCK

    barrier = pltpu.get_barrier_semaphore()
    pl.semaphore_signal(barrier, inc=1, device_id={"head": other}, device_id_type=MESH)
    greeted = jnp.int32(1)
    for ok, device in greet:
        @pl.when(ok)
        def _(device=device):
            pl.semaphore_signal(barrier, inc=1, device_id={"seq": device}, device_id_type=MESH)

        greeted = greeted + jnp.where(ok, 1, 0).astype(jnp.int32)
    pl.semaphore_wait(barrier, greeted)

    def copy_of(entry):
        ok, device, source, landing, out_sem, in_sem = entry
        return pltpu.make_async_remote_copy(
            src_ref=source, dst_ref=landing, send_sem=send_sem.at[out_sem], recv_sem=recv_sem.at[in_sem],
            device_id={"seq": device}, device_id_type=MESH,
        )

    def start_all(entries):
        for entry in entries:
            @pl.when(entry[0])
            def _(entry=entry):
                copy_of(entry).start()

    def start_whole(level):
        for ok, landing, in_sem in gathered[level]:
            pltpu.make_async_remote_copy(
                src_ref=landing, dst_ref=landing, send_sem=send_sem.at[in_sem], recv_sem=recv_sem.at[in_sem],
                device_id={"seq": (s + 1) % seq_count}, device_id_type=MESH,
            ).wait_recv()
        start_all(sends[level])

    def wait_level(level):
        for ok, landing, in_sem in arrivals[level]:
            @pl.when(ok)
            def _(landing=landing, in_sem=in_sem):
                pltpu.make_async_remote_copy(
                    src_ref=landing, dst_ref=landing, send_sem=send_sem.at[in_sem], recv_sem=recv_sem.at[in_sem],
                    device_id={"seq": (s + 1) % seq_count}, device_id_type=MESH,
                ).wait_recv()

            @pl.when(jnp.logical_not(ok))
            def _(landing=landing):
                landing[...] = jnp.zeros(landing.shape, landing.dtype)

    chunk = 16 << levels
    load_kv.wait()

    def average(level, chunk=chunk):
        rows = chunk >> level
        position = lax.broadcasted_iota(jnp.int32, (rows, chunk), 1) >> level
        match = position == lax.broadcasted_iota(jnp.int32, (rows, chunk), 0)
        return jnp.where(match, 1.0 / (1 << level), 0.0).astype(jnp.bfloat16)

    def shrink(level, matrix, kv_row, count, to_ref, to_row):
        tokens_at, at = pl.ds(kv_row, count), pl.ds(to_row, count >> level)
        to_ref[at, 0:width] = jnp.dot(
            matrix, kv0[tokens_at, 0:width], preferred_element_type=jnp.float32
        ).astype(jnp.bfloat16)
        to_ref[at, width : 2 * width] = (
            jnp.dot(matrix, kv0[tokens_at, width : 2 * width], preferred_element_type=jnp.float32)
            * float(1 << level)
        ).astype(jnp.bfloat16)

    for level in range(levels, 0, -1):
        rows = chunk >> level
        matrix = average(level)
        place = s % spread(level) if level > 1 else 0
        for c in range(tokens // chunk):
            to_row = own_row[level] + place * row_count[level] + c * rows
            if level > 1:
                to_row = pl.multiple_of(to_row, rows)
            shrink(level, matrix, BLOCK + c * chunk, chunk, own, to_row)
        if level > 2:
            start_all(gathers[level])
            if level == 3:
                start_all(sends[0])
        elif level == 2:
            start_all(sends[level])
    for level in range(levels, 2, -1):
        start_whole(level)
    load_q.wait()
    for level in range(1, levels + 1):
        rows = chunk >> level
        matrix = average(level)
        for c in range(tokens // chunk):
            qc[pl.ds(start_row[level] + c * rows, rows), :] = jnp.dot(
                matrix, q0[pl.ds(c * chunk, chunk), :], preferred_element_type=jnp.float32
            ).astype(jnp.bfloat16)

    def bias_of(oks):
        column = lax.broadcasted_iota(jnp.int32, (1, 3 * BLOCK), 1)
        b = [jnp.where(ok, 0.0, NEG).astype(jnp.float32) for ok in oks]
        return jnp.where(column < BLOCK, b[0], jnp.where(column < 2 * BLOCK, b[1], b[2]))

    def attend(level, q_ref, q_row, rows, kv_ref, pieces, bias, to_row):
        def one_head(head):
            cols = pl.ds(head * BLOCK, BLOCK)
            vcols = pl.ds(width + head * BLOCK, BLOCK)
            keys = jnp.concatenate([kv_ref[pl.ds(a, n), cols] for a, n in pieces], axis=0)
            values = jnp.concatenate([kv_ref[pl.ds(a, n), vcols] for a, n in pieces], axis=0)
            scores = lax.dot_general(
                q_ref[pl.ds(q_row, rows), cols], keys, (((1,), (1,)), ((), ())), preferred_element_type=jnp.float32
            ) * scale
            if bias is not None:
                scores = scores + bias
            top = jnp.max(scores, axis=1, keepdims=True)
            weights = jnp.exp(scores - top)
            sums = jnp.sum(weights, axis=1, keepdims=True) * float(1 << level)
            at = pl.ds(to_row, rows)
            num[at, cols] = jnp.dot(weights.astype(jnp.bfloat16), values, preferred_element_type=jnp.float32)
            peak[at, cols] = jnp.broadcast_to(top, (rows, BLOCK))
            den[at, cols] = jnp.broadcast_to(sums, (rows, BLOCK))

        for head in range(heads):
            one_head(head)

    yes = s >= 0
    for i in range(1, blocks - 1):
        attend(0, q0, i * BLOCK, BLOCK, kv0, [(i * BLOCK, 3 * BLOCK)], None, i * BLOCK)
    wait_level(0)
    start_all(sends[1])
    last = blocks - 1
    attend(0, q0, 0, BLOCK, kv0, [(0, 3 * BLOCK)], bias_of([left_ok, yes, yes]), 0)
    attend(
        0, q0, last * BLOCK, BLOCK, kv0, [(last * BLOCK, 3 * BLOCK)], bias_of([yes, yes, right_ok]), last * BLOCK
    )
    for level in range(2, levels + 1):
        wait_level(level)
        attend(
            level, qc, start_row[level], row_count[level], far, [(far_row[level], 3 * BLOCK)],
            bias_of(slot_ok[level]), term_row[level],
        )
    wait_level(1)
    matrix = average(1, BLOCK)
    shrink(1, matrix, 0, BLOCK, far, n1 - edge)
    shrink(1, matrix, BLOCK + tokens, BLOCK, far, n1)
    attend(
        1, qc, 0, BLOCK, far, [(0, BLOCK), (n1, n1)], bias_of([left_ok, right_ok, right_ok]), term_row[1]
    )
    attend(
        1, qc, BLOCK, BLOCK, far, [(0, n1), (n1 + BLOCK, BLOCK)], bias_of([left_ok, left_ok, right_ok]),
        term_row[1] + BLOCK,
    )

    for head in range(heads):
        cols = pl.ds(head * BLOCK, BLOCK)

        def terms(level):
            at = pl.ds(term_row[level], row_count[level])
            return peak[at, cols], num[at, cols], den[at, cols]

        def merge(a, b):
            m = jnp.maximum(a[0], b[0])
            fa, fb = jnp.exp(a[0] - m), jnp.exp(b[0] - m)
            return m, fa * a[1] + fb * b[1], fa * a[2] + fb * b[2]

        state = terms(levels)
        if extra:
            state = merge(state, (xm_ref[:, cols], xn_ref[:, cols], xr_ref[:, cols]))
        for level in range(levels - 1, -1, -1):
            n = row_count[level + 1]
            for ref, value in zip((tm, tn, tr), state):
                ref[pl.ds(0, n, 2), :] = value
                ref[pl.ds(1, n, 2), :] = value
            wide = tuple(ref[pl.ds(0, 2 * n), :] for ref in (tm, tn, tr))
            state = merge(wide, terms(level))
        att[:, cols] = (state[1] / state[2]).astype(jnp.bfloat16)

    load_w.wait()
    theirs = pl.ds(pl.multiple_of(other * half, BLOCK), half)
    ours = pl.ds(pl.multiple_of(h * half, BLOCK), half)

    def share(c):
        at = pl.ds(c * BLOCK, BLOCK)
        return pltpu.make_async_remote_copy(
            src_ref=psend.at[at], dst_ref=precv.at[at], send_sem=psend_sem.at[c], recv_sem=precv_sem.at[c],
            device_id={"head": other}, device_id_type=MESH,
        )

    for c in range(blocks):
        at = pl.ds(c * BLOCK, BLOCK)
        psend[at, :] = jnp.dot(att[at, :], w[:, theirs], preferred_element_type=jnp.float32).astype(jnp.bfloat16)
        share(c).start()
    for c in range(blocks):
        at = pl.ds(c * BLOCK, BLOCK)
        kept = jnp.dot(att[at, :], w[:, ours], preferred_element_type=jnp.float32).astype(jnp.bfloat16)
        share(c).wait_recv()
        out_ref[at, :] = (kept.astype(jnp.float32) + precv[at, :].astype(jnp.float32)).astype(jnp.bfloat16)
    for c in range(blocks):
        share(c).wait_send()
    for level in range(levels + 1):
        for entry in gathers.get(level, []) + sends[level]:
            @pl.when(entry[0])
            def _(entry=entry):
                copy_of(entry).wait_send()


def upper_terms(query_rows, key_rows, value_rows, first, top, rows_at):
    seq_count = lax.axis_size("seq")
    device_index = lax.axis_index("seq")
    scale = float(query_rows.shape[2]) ** (-0.5)
    merged = None
    for level_index in range(first, top + 1):
        queries = coarsen(query_rows, level_index, True)
        piece = jnp.stack([coarsen(key_rows, level_index, True), coarsen(value_rows, level_index, False)])
        whole_block = assemble_one(piece, level_index - 2, device_index)
        group = 1 << level_index - 2
        before_two = shifted(whole_block, "seq", 2 * group)
        after_two = shifted(whole_block, "seq", -2 * group)
        block_index = device_index // group
        outgoing = jnp.where(block_index % 2 == 0, before_two, after_two)
        third_block = partner_2(outgoing, "seq", level_index - 2)
        level_keys = jnp.concatenate([before_two, after_two, third_block], axis=1)[:, None]
        valid = slot_masks(jnp.reshape(block_index, (1,)), seq_count // group, level_index, BLOCK)
        terms = level_attend(queries[None], level_keys[0], level_keys[1], valid, level_index, scale)
        terms = [jnp.repeat(term, rows_at // term.shape[0], axis=0) for term in terms]
        if merged is None:
            merged = terms
        else:
            m = jnp.maximum(merged[0], terms[0])
            fa, fb = jnp.exp(merged[0] - m), jnp.exp(terms[0] - m)
            merged = [
                m,
                fa[:, :, None] * merged[1] + fb[:, :, None] * terms[1],
                fa * merged[2] + fb * terms[2],
            ]
    flat = (rows_at, merged[1].shape[1] * merged[1].shape[2])
    wide = [jnp.broadcast_to(x[:, :, None], merged[1].shape).reshape(flat) for x in (merged[0], merged[2])]
    return [wide[0], merged[1].reshape(flat), wide[1]]


def per_device(query_rows, key_rows, value_rows, out_weight):
    seq_count = lax.axis_size("seq")
    tokens, heads, head_size = query_rows.shape
    width = heads * head_size
    features = out_weight.shape[2]
    half = features // lax.axis_size("head")
    top = seq_count.bit_length() - 1
    levels = min(top, KERNEL_TOP)
    extra = []
    if top > levels:
        extra = upper_terms(query_rows, key_rows, value_rows, levels + 1, top, tokens >> levels)
    queries = query_rows.reshape(tokens, width)
    pairs = jnp.concatenate([key_rows.reshape(tokens, width), value_rows.reshape(tokens, width)], axis=1)
    weight = out_weight.reshape(width, features)
    coarse = sum(tokens >> level for level in range(1, levels + 1))
    far_rows = 2 * (tokens >> 1) + 3 * BLOCK * (levels - 1)
    copies = 4 + sum(2 + spread(level) for level in range(2, levels + 1))
    blocks = tokens // BLOCK
    bf16, f32 = jnp.bfloat16, jnp.float32
    return pl.pallas_call(
        functools.partial(layer_kernel, seq_count, levels, bool(extra)),
        out_shape=jax.ShapeDtypeStruct((tokens, half), bf16),
        in_specs=[pl.BlockSpec(memory_space=pl.ANY)] * 3 + [pl.BlockSpec(memory_space=pltpu.VMEM)] * len(extra),
        out_specs=pl.BlockSpec(memory_space=pltpu.VMEM),
        scratch_shapes=[
            pltpu.VMEM((tokens, width), bf16),
            pltpu.VMEM((tokens + 2 * BLOCK, 2 * width), bf16),
            pltpu.VMEM((width, features), bf16),
            pltpu.VMEM((tokens // 2 + BLOCK * (levels - 1), 2 * width), bf16),
            pltpu.VMEM((coarse, width), bf16),
            pltpu.VMEM((far_rows, 2 * width), bf16),
            pltpu.VMEM((tokens, width), bf16),
            pltpu.VMEM((tokens + coarse, width), f32),
            pltpu.VMEM((tokens + coarse, width), f32),
            pltpu.VMEM((tokens + coarse, width), f32),
            pltpu.VMEM((tokens, BLOCK), f32),
            pltpu.VMEM((tokens, BLOCK), f32),
            pltpu.VMEM((tokens, BLOCK), f32),
            pltpu.VMEM((tokens, half), bf16),
            pltpu.VMEM((tokens, half), bf16),
            pltpu.SemaphoreType.DMA((3,)),
            pltpu.SemaphoreType.DMA((copies,)),
            pltpu.SemaphoreType.DMA((copies,)),
            pltpu.SemaphoreType.DMA((blocks,)),
            pltpu.SemaphoreType.DMA((blocks,)),
        ],
        compiler_params=pltpu.CompilerParams(
            collective_id=0, has_side_effects=True, vmem_limit_bytes=48 * 2**20
        ),
        cost_estimate=pl.CostEstimate(flops=3 * 10**9, bytes_accessed=6 * 2**20, transcendentals=2 * 10**6),
    )(queries, pairs, weight, *extra)


def solution(mesh):
    return jax.shard_map(
        per_device,
        mesh=mesh,
        in_specs=(
            P("seq", "head", None),
            P("seq", "head", None),
            P("seq", "head", None),
            P("head", None, None),
        ),
        out_specs=P("seq", "head"),
        check_vma=False,
    )
```

```python
import functools

import jax
import jax.numpy as jnp
from jax import lax
from jax.experimental import pallas as pl
from jax.experimental.pallas import tpu as pltpu
from jax.sharding import PartitionSpec as P

BLOCK = 128


def partner_2(value, axis, distance):
    mask = 2**distance
    pairs = [(source, source ^ mask) for source in range(lax.axis_size(axis))]
    return lax.ppermute(value, axis, pairs)


def shifted(value, axis, steps):
    count = lax.axis_size(axis)
    initial, last = (max(0, -steps), min(count, count - steps))
    return lax.ppermute(value, axis, [(source, source + steps) for source in range(initial, last)])


def coarsen(source, level_index, average):
    count = source.shape[0] >> level_index
    grouped = source.astype(jnp.float32).reshape((count, 1 << level_index) + source.shape[1:])
    summed = jnp.sum(grouped, axis=1)
    if average:
        summed = summed / float(1 << level_index)
    return summed.astype(jnp.bfloat16)


def slot_targets(block_index, level_index):
    if level_index == 0:
        return [block_index - 1, block_index, block_index + 1]
    return [
        block_index - 2,
        block_index + 2,
        jnp.where(block_index % 2 == 0, block_index + 3, block_index - 3),
    ]


def slot_masks(block_index, block_total, level_index, width):
    targets = slot_targets(block_index, level_index)
    return jnp.concatenate(
        [
            jnp.repeat(((target >= 0) & (target < block_total))[:, None], width, axis=1)
            for target in targets
        ],
        axis=1,
    )


def level_attend(query_blocks, key_blocks, value_blocks, valid, level_index, scale):
    scores = (
        jnp.einsum("nqhd,nkhd->nhqk", query_blocks, key_blocks, preferred_element_type=jnp.float32)
        * scale
    )
    scores = jnp.where(valid[:, None, None, :], scores, -jnp.inf)
    row_peak = jnp.max(scores, axis=3, keepdims=True)
    weights = jnp.exp(scores - row_peak)
    denominator = float(1 << level_index) * jnp.sum(weights, axis=3)
    numerator = jnp.einsum(
        "nhqk,nkhd->nqhd",
        weights.astype(jnp.bfloat16),
        value_blocks,
        preferred_element_type=jnp.float32,
    )
    block_count = query_blocks.shape[0]
    row_count = query_blocks.shape[1]
    peak_rows = jnp.transpose(row_peak[..., 0], (0, 2, 1)).reshape(block_count * row_count, -1)
    denominator_rows = jnp.transpose(denominator, (0, 2, 1)).reshape(block_count * row_count, -1)
    numerator_rows = numerator.reshape(
        block_count * row_count, numerator.shape[2], numerator.shape[3]
    )
    return (peak_rows, numerator_rows, denominator_rows)


def upper_half(device_index, bit):
    return device_index // (1 << bit) % 2 == 1


def assemble_one(piece, bit_count, device_index):
    for bit in range(bit_count):
        partner = partner_2(piece, "seq", bit)
        piece = jnp.where(
            upper_half(device_index, bit),
            jnp.concatenate([partner, piece], axis=1),
            jnp.concatenate([piece, partner], axis=1),
        )
    return piece


MESH = pl.DeviceIdType.MESH
NEG = -1e30
KERNEL_TOP = 4


def spread(level):
    return 1 << (level - 2)


def layer_kernel(seq_count, levels, extra, *refs):
    q_hbm, kv_hbm, w_hbm = refs[:3]
    refs = refs[3:]
    if extra:
        xm_ref, xn_ref, xr_ref = refs[:3]
        refs = refs[3:]
    out_ref = refs[0]
    q0, kv0, w, own, qc, far, att, peak, num, den, tm, tn, tr, psend, precv = refs[1:16]
    load_sem, send_sem, recv_sem, psend_sem, precv_sem = refs[16:]
    tokens, width = q_hbm.shape
    heads = width // BLOCK
    blocks = tokens // BLOCK
    half = out_ref.shape[1]
    scale = float(BLOCK) ** (-0.5)
    s = lax.axis_index("seq")
    h = lax.axis_index("head")
    other = 1 - h

    row_count = [tokens >> level for level in range(levels + 1)]
    start_row = [sum(row_count[1:level]) for level in range(levels + 1)]
    term_row = [sum(row_count[:level]) for level in range(levels + 1)]

    load_kv = pltpu.make_async_copy(kv_hbm, kv0.at[pl.ds(BLOCK, tokens)], load_sem.at[0])
    load_q = pltpu.make_async_copy(q_hbm, q0, load_sem.at[1])
    load_w = pltpu.make_async_copy(w_hbm, w, load_sem.at[2])
    load_kv.start()
    load_q.start()
    load_w.start()

    sends = {level: [] for level in range(levels + 1)}
    arrivals = {level: [] for level in range(levels + 1)}
    greet = []
    left_ok, right_ok = s >= 1, s + 1 < seq_count
    greet += [(left_ok, s - 1), (right_ok, s + 1)]
    sends[0] += [
        (right_ok, s + 1, kv_hbm.at[pl.ds(tokens - BLOCK, BLOCK)], kv0.at[pl.ds(0, BLOCK)], 0, 0),
        (left_ok, s - 1, kv_hbm.at[pl.ds(0, BLOCK)], kv0.at[pl.ds(BLOCK + tokens, BLOCK)], 1, 1),
    ]
    arrivals[0] += [(left_ok, sends[0][0][3], 0), (right_ok, sends[0][1][3], 1)]
    n1 = row_count[1]
    edge = BLOCK // 2
    sends[1] += [
        (right_ok, s + 1, own.at[pl.ds(0, n1 - edge)], far.at[pl.ds(0, n1 - edge)], 2, 2),
        (left_ok, s - 1, own.at[pl.ds(edge, n1 - edge)], far.at[pl.ds(n1 + edge, n1 - edge)], 3, 3),
    ]
    arrivals[1] += [(left_ok, sends[1][0][3], 2), (right_ok, sends[1][1][3], 3)]
    sem = 4
    far_row = {1: 0}
    own_row = {1: 0}
    gathers = {level: [] for level in range(2, levels + 1)}
    gathered = {level: [] for level in range(2, levels + 1)}
    relays = {level: [] for level in range(2, levels + 1)}
    relayed = {level: [] for level in range(2, levels + 1)}
    base = 2 * n1
    slot_ok = {}
    for level in range(2, levels + 1):
        far_row[level] = base
        group = spread(level)
        rows = row_count[level]
        block, place = s // group, s % group
        odd = block % 2
        total = seq_count // group
        own_row[level] = n1 + (level - 2) * BLOCK
        third = block + 3 - 6 * odd
        sources = [block - 2, block + 2, third]
        targets = [block + 2, block - 2, third]

        def piece(at, level=level, rows=rows):
            return own.at[pl.ds(pl.multiple_of(own_row[level] + at * rows, rows), rows)]

        peers = [block * group + (place + step) % group for step in range(1, group)]
        direct = group > 2
        for step, device in enumerate(peers, 1):
            greet.append((s >= 0, device))
            if not direct:
                gathers[level].append((s >= 0, device, piece(place), piece(place), sem, sem))
                gathered[level].append((s >= 0, piece((place + group - step) % group), sem))
                sem += 1
        oks = []
        whole = own.at[pl.ds(own_row[level], BLOCK)]
        for slot in range(3):
            to_ok = (targets[slot] >= 0) & (targets[slot] < total)
            from_ok = (sources[slot] >= 0) & (sources[slot] < total)
            oks.append(from_ok)
            device = targets[slot] * group + place
            greet.append((to_ok, device))
            if not direct:
                landing = far.at[pl.ds(base + slot * BLOCK, BLOCK)]
                sends[level].append((to_ok, device, whole, landing, sem, sem))
                arrivals[level].append((from_ok, landing, sem))
                sem += 1
                continue

            def part(at, first=base + slot * BLOCK, rows=rows):
                return far.at[pl.ds(pl.multiple_of(first + at * rows, rows), rows)]

            sends[level].append((to_ok, device, piece(place), part(place), sem, sem))
            relayed[level].append((from_ok, part(place), sem))
            sem += 1
            for step, peer in enumerate(peers, 1):
                relays[level].append((from_ok, peer, part(place), part(place), sem, sem))
                arrivals[level].append((from_ok, part((place + group - step) % group), sem))
                sem += 1
        slot_ok[level] = oks
        base += 3 * BLOCK

    barrier = pltpu.get_barrier_semaphore()
    pl.semaphore_signal(barrier, inc=1, device_id={"head": other}, device_id_type=MESH)
    greeted = jnp.int32(1)
    for ok, device in greet:
        @pl.when(ok)
        def _(device=device):
            pl.semaphore_signal(barrier, inc=1, device_id={"seq": device}, device_id_type=MESH)

        greeted = greeted + jnp.where(ok, 1, 0).astype(jnp.int32)
    pl.semaphore_wait(barrier, greeted)

    def copy_of(entry):
        ok, device, source, landing, out_sem, in_sem = entry
        return pltpu.make_async_remote_copy(
            src_ref=source, dst_ref=landing, send_sem=send_sem.at[out_sem], recv_sem=recv_sem.at[in_sem],
            device_id={"seq": device}, device_id_type=MESH,
        )

    def start_all(entries):
        for entry in entries:
            @pl.when(entry[0])
            def _(entry=entry):
                copy_of(entry).start()

    def start_whole(level):
        for ok, landing, in_sem in gathered[level]:
            pltpu.make_async_remote_copy(
                src_ref=landing, dst_ref=landing, send_sem=send_sem.at[in_sem], recv_sem=recv_sem.at[in_sem],
                device_id={"seq": (s + 1) % seq_count}, device_id_type=MESH,
            ).wait_recv()
        start_all(sends[level])

    def wait_level(level):
        wait_all(arrivals[level])

    def wait_all(entries):
        for ok, landing, in_sem in entries:
            @pl.when(ok)
            def _(landing=landing, in_sem=in_sem):
                pltpu.make_async_remote_copy(
                    src_ref=landing, dst_ref=landing, send_sem=send_sem.at[in_sem], recv_sem=recv_sem.at[in_sem],
                    device_id={"seq": (s + 1) % seq_count}, device_id_type=MESH,
                ).wait_recv()

            @pl.when(jnp.logical_not(ok))
            def _(landing=landing):
                landing[...] = jnp.zeros(landing.shape, landing.dtype)

    chunk = 16 << levels
    load_kv.wait()

    def average(level, chunk=chunk):
        rows = chunk >> level
        position = lax.broadcasted_iota(jnp.int32, (rows, chunk), 1) >> level
        match = position == lax.broadcasted_iota(jnp.int32, (rows, chunk), 0)
        return jnp.where(match, 1.0 / (1 << level), 0.0).astype(jnp.bfloat16)

    def shrink(level, matrix, kv_row, count, to_ref, to_row):
        tokens_at, at = pl.ds(kv_row, count), pl.ds(to_row, count >> level)
        to_ref[at, 0:width] = jnp.dot(
            matrix, kv0[tokens_at, 0:width], preferred_element_type=jnp.float32
        ).astype(jnp.bfloat16)
        to_ref[at, width : 2 * width] = (
            jnp.dot(matrix, kv0[tokens_at, width : 2 * width], preferred_element_type=jnp.float32)
            * float(1 << level)
        ).astype(jnp.bfloat16)

    for level in range(levels, 0, -1):
        rows = chunk >> level
        matrix = average(level)
        place = s % spread(level) if level > 1 else 0
        for c in range(tokens // chunk):
            to_row = own_row[level] + place * row_count[level] + c * rows
            if level > 1:
                to_row = pl.multiple_of(to_row, rows)
            shrink(level, matrix, BLOCK + c * chunk, chunk, own, to_row)
        if level > 2:
            start_all(gathers[level] or sends[level])
            if level == 3:
                start_all(sends[0])
        elif level == 2:
            start_all(sends[level])
    for level in range(levels, 2, -1):
        if gathers[level]:
            start_whole(level)
    load_q.wait()
    for level in range(1, levels + 1):
        rows = chunk >> level
        matrix = average(level)
        for c in range(tokens // chunk):
            qc[pl.ds(start_row[level] + c * rows, rows), :] = jnp.dot(
                matrix, q0[pl.ds(c * chunk, chunk), :], preferred_element_type=jnp.float32
            ).astype(jnp.bfloat16)

    def bias_of(oks):
        column = lax.broadcasted_iota(jnp.int32, (1, 3 * BLOCK), 1)
        b = [jnp.where(ok, 0.0, NEG).astype(jnp.float32) for ok in oks]
        return jnp.where(column < BLOCK, b[0], jnp.where(column < 2 * BLOCK, b[1], b[2]))

    def attend(level, q_ref, q_row, rows, kv_ref, pieces, bias, to_row):
        def one_head(head):
            cols = pl.ds(head * BLOCK, BLOCK)
            vcols = pl.ds(width + head * BLOCK, BLOCK)
            keys = jnp.concatenate([kv_ref[pl.ds(a, n), cols] for a, n in pieces], axis=0)
            values = jnp.concatenate([kv_ref[pl.ds(a, n), vcols] for a, n in pieces], axis=0)
            scores = lax.dot_general(
                q_ref[pl.ds(q_row, rows), cols], keys, (((1,), (1,)), ((), ())), preferred_element_type=jnp.float32
            ) * scale
            if bias is not None:
                scores = scores + bias
            top = jnp.max(scores, axis=1, keepdims=True)
            weights = jnp.exp(scores - top)
            sums = jnp.sum(weights, axis=1, keepdims=True) * float(1 << level)
            at = pl.ds(to_row, rows)
            num[at, cols] = jnp.dot(weights.astype(jnp.bfloat16), values, preferred_element_type=jnp.float32)
            peak[at, cols] = jnp.broadcast_to(top, (rows, BLOCK))
            den[at, cols] = jnp.broadcast_to(sums, (rows, BLOCK))

        for head in range(heads):
            one_head(head)

    yes = s >= 0
    for i in range(1, blocks - 1):
        attend(0, q0, i * BLOCK, BLOCK, kv0, [(i * BLOCK, 3 * BLOCK)], None, i * BLOCK)
    for level in range(levels, 2, -1):
        wait_all(relayed[level])
        start_all(relays[level])
    wait_level(0)
    start_all(sends[1])
    last = blocks - 1
    attend(0, q0, 0, BLOCK, kv0, [(0, 3 * BLOCK)], bias_of([left_ok, yes, yes]), 0)
    attend(
        0, q0, last * BLOCK, BLOCK, kv0, [(last * BLOCK, 3 * BLOCK)], bias_of([yes, yes, right_ok]), last * BLOCK
    )
    for level in range(2, levels + 1):
        wait_level(level)
        attend(
            level, qc, start_row[level], row_count[level], far, [(far_row[level], 3 * BLOCK)],
            bias_of(slot_ok[level]), term_row[level],
        )
    def terms(level, cols):
        at = pl.ds(term_row[level], row_count[level])
        return peak[at, cols], num[at, cols], den[at, cols]

    def merge(a, b):
        m = jnp.maximum(a[0], b[0])
        fa, fb = jnp.exp(a[0] - m), jnp.exp(b[0] - m)
        return m, fa * a[1] + fb * b[1], fa * a[2] + fb * b[2]

    def refine(state, high, low, cols):
        for level in range(high - 1, low - 1, -1):
            n = row_count[level + 1]
            for ref, value in zip((tm, tn, tr), state):
                ref[pl.ds(0, n, 2), :] = value
                ref[pl.ds(1, n, 2), :] = value
            wide = tuple(ref[pl.ds(0, 2 * n), :] for ref in (tm, tn, tr))
            state = merge(wide, terms(level, cols))
        return state

    for head in range(heads):
        cols = pl.ds(head * BLOCK, BLOCK)
        state = terms(levels, cols)
        if extra:
            state = merge(state, (xm_ref[:, cols], xn_ref[:, cols], xr_ref[:, cols]))
        at = pl.ds(term_row[2], row_count[2])
        peak[at, cols], num[at, cols], den[at, cols] = refine(state, levels, 2, cols)

    wait_level(1)
    matrix = average(1, BLOCK)
    shrink(1, matrix, 0, BLOCK, far, n1 - edge)
    shrink(1, matrix, BLOCK + tokens, BLOCK, far, n1)
    attend(
        1, qc, 0, BLOCK, far, [(0, BLOCK), (n1, n1)], bias_of([left_ok, right_ok, right_ok]), term_row[1]
    )
    attend(
        1, qc, BLOCK, BLOCK, far, [(0, n1), (n1 + BLOCK, BLOCK)], bias_of([left_ok, left_ok, right_ok]),
        term_row[1] + BLOCK,
    )

    for head in range(heads):
        cols = pl.ds(head * BLOCK, BLOCK)
        state = refine(terms(2, cols), 2, 0, cols)
        att[:, cols] = (state[1] / state[2]).astype(jnp.bfloat16)

    load_w.wait()
    theirs = pl.ds(pl.multiple_of(other * half, BLOCK), half)
    ours = pl.ds(pl.multiple_of(h * half, BLOCK), half)

    def share(c):
        at = pl.ds(c * BLOCK, BLOCK)
        return pltpu.make_async_remote_copy(
            src_ref=psend.at[at], dst_ref=precv.at[at], send_sem=psend_sem.at[c], recv_sem=precv_sem.at[c],
            device_id={"head": other}, device_id_type=MESH,
        )

    for c in range(blocks):
        at = pl.ds(c * BLOCK, BLOCK)
        psend[at, :] = jnp.dot(att[at, :], w[:, theirs], preferred_element_type=jnp.float32).astype(jnp.bfloat16)
        share(c).start()
    for c in range(blocks):
        at = pl.ds(c * BLOCK, BLOCK)
        kept = jnp.dot(att[at, :], w[:, ours], preferred_element_type=jnp.float32).astype(jnp.bfloat16)
        share(c).wait_recv()
        out_ref[at, :] = (kept.astype(jnp.float32) + precv[at, :].astype(jnp.float32)).astype(jnp.bfloat16)
    for c in range(blocks):
        share(c).wait_send()
    for level in range(levels + 1):
        for entry in gathers.get(level, []) + relays.get(level, []) + sends[level]:
            @pl.when(entry[0])
            def _(entry=entry):
                copy_of(entry).wait_send()


def upper_terms(query_rows, key_rows, value_rows, first, top, rows_at):
    seq_count = lax.axis_size("seq")
    device_index = lax.axis_index("seq")
    scale = float(query_rows.shape[2]) ** (-0.5)
    merged = None
    for level_index in range(first, top + 1):
        queries = coarsen(query_rows, level_index, True)
        piece = jnp.stack([coarsen(key_rows, level_index, True), coarsen(value_rows, level_index, False)])
        whole_block = assemble_one(piece, level_index - 2, device_index)
        group = 1 << level_index - 2
        before_two = shifted(whole_block, "seq", 2 * group)
        after_two = shifted(whole_block, "seq", -2 * group)
        block_index = device_index // group
        outgoing = jnp.where(block_index % 2 == 0, before_two, after_two)
        third_block = partner_2(outgoing, "seq", level_index - 2)
        level_keys = jnp.concatenate([before_two, after_two, third_block], axis=1)[:, None]
        valid = slot_masks(jnp.reshape(block_index, (1,)), seq_count // group, level_index, BLOCK)
        terms = level_attend(queries[None], level_keys[0], level_keys[1], valid, level_index, scale)
        terms = [jnp.repeat(term, rows_at // term.shape[0], axis=0) for term in terms]
        if merged is None:
            merged = terms
        else:
            m = jnp.maximum(merged[0], terms[0])
            fa, fb = jnp.exp(merged[0] - m), jnp.exp(terms[0] - m)
            merged = [
                m,
                fa[:, :, None] * merged[1] + fb[:, :, None] * terms[1],
                fa * merged[2] + fb * terms[2],
            ]
    flat = (rows_at, merged[1].shape[1] * merged[1].shape[2])
    wide = [jnp.broadcast_to(x[:, :, None], merged[1].shape).reshape(flat) for x in (merged[0], merged[2])]
    return [wide[0], merged[1].reshape(flat), wide[1]]


def per_device(query_rows, key_rows, value_rows, out_weight):
    seq_count = lax.axis_size("seq")
    tokens, heads, head_size = query_rows.shape
    width = heads * head_size
    features = out_weight.shape[2]
    half = features // lax.axis_size("head")
    top = seq_count.bit_length() - 1
    levels = min(top, KERNEL_TOP)
    extra = []
    if top > levels:
        extra = upper_terms(query_rows, key_rows, value_rows, levels + 1, top, tokens >> levels)
    queries = query_rows.reshape(tokens, width)
    pairs = jnp.concatenate([key_rows.reshape(tokens, width), value_rows.reshape(tokens, width)], axis=1)
    weight = out_weight.reshape(width, features)
    coarse = sum(tokens >> level for level in range(1, levels + 1))
    far_rows = 2 * (tokens >> 1) + 3 * BLOCK * (levels - 1)
    copies = 4 + sum(3 * spread(level) for level in range(2, levels + 1))
    blocks = tokens // BLOCK
    bf16, f32 = jnp.bfloat16, jnp.float32
    return pl.pallas_call(
        functools.partial(layer_kernel, seq_count, levels, bool(extra)),
        out_shape=jax.ShapeDtypeStruct((tokens, half), bf16),
        in_specs=[pl.BlockSpec(memory_space=pl.ANY)] * 3 + [pl.BlockSpec(memory_space=pltpu.VMEM)] * len(extra),
        out_specs=pl.BlockSpec(memory_space=pltpu.VMEM),
        scratch_shapes=[
            pltpu.VMEM((tokens, width), bf16),
            pltpu.VMEM((tokens + 2 * BLOCK, 2 * width), bf16),
            pltpu.VMEM((width, features), bf16),
            pltpu.VMEM((tokens // 2 + BLOCK * (levels - 1), 2 * width), bf16),
            pltpu.VMEM((coarse, width), bf16),
            pltpu.VMEM((far_rows, 2 * width), bf16),
            pltpu.VMEM((tokens, width), bf16),
            pltpu.VMEM((tokens + coarse, width), f32),
            pltpu.VMEM((tokens + coarse, width), f32),
            pltpu.VMEM((tokens + coarse, width), f32),
            pltpu.VMEM((tokens, BLOCK), f32),
            pltpu.VMEM((tokens, BLOCK), f32),
            pltpu.VMEM((tokens, BLOCK), f32),
            pltpu.VMEM((tokens, half), bf16),
            pltpu.VMEM((tokens, half), bf16),
            pltpu.SemaphoreType.DMA((3,)),
            pltpu.SemaphoreType.DMA((copies,)),
            pltpu.SemaphoreType.DMA((copies,)),
            pltpu.SemaphoreType.DMA((blocks,)),
            pltpu.SemaphoreType.DMA((blocks,)),
        ],
        compiler_params=pltpu.CompilerParams(
            collective_id=0, has_side_effects=True, vmem_limit_bytes=48 * 2**20
        ),
        cost_estimate=pl.CostEstimate(flops=3 * 10**9, bytes_accessed=6 * 2**20, transcendentals=2 * 10**6),
    )(queries, pairs, weight, *extra)


def solution(mesh):
    return jax.shard_map(
        per_device,
        mesh=mesh,
        in_specs=(
            P("seq", "head", None),
            P("seq", "head", None),
            P("seq", "head", None),
            P("head", None, None),
        ),
        out_specs=P("seq", "head"),
        check_vma=False,
    )
```
